32 devices in a mesh: ctx: 8 (over z, core), dp: 4 (over y, x).
Axes of the slice: x: 2, y: 2, z: 4, core: 2. Of those that a mesh axis runs over, the one named last changes fastest.
Arguments:
- stream: bfloat16 [3, 1024, 8192], P(None, 'ctx', 'dp'), may hold values from -6 to 6
- short_taps: float32 [3, 3, 8192], replicated, may hold values from -3.5 to 3.5
- decay_rate: float32 [16, 512], P('dp'), may hold values from 0.0001953125 to 0.1
- residue: float32 [16, 512], P('dp'), may hold values from -0.4472136 to 0.4472136
Outputs:
- gated_output: bfloat16 [1024, 8192], P('ctx', 'dp')
The draws below stay inside these ranges and needn't reach their ends.
All inputs are finite; a program needn't handle non-finite values.
Results may differ from the reference program's by a relative error of at most 0.002.
Values may be sent and summed in bfloat16 or wider, within the bound.
A program may use at most 128 MiB of HBM per device.

```python
import math
import jax
import jax.numpy as jnp
from jax import lax

D = 8192
GROUP = 16
ORDER = 16
TAPS = 3
G = 512
TOKENS = 1024


def filter_pair(key):
    base_key = jax.random.fold_in(key, 31)
    pick_key, rate_key, signs_key = jax.random.split(base_key, 3)
    slow_share = 0.5
    slow_pick = jax.random.bernoulli(pick_key, slow_share, (ORDER, G))
    unit_draw = jax.random.uniform(rate_key, (ORDER, G), jnp.float32)
    slow_rate = jnp.exp(jnp.log(0.2 / TOKENS) + unit_draw * jnp.log(10.0))
    fast_rate = jnp.exp(jnp.log(0.02) + unit_draw * jnp.log(5.0))
    rate_value = jnp.where(slow_pick, slow_rate, fast_rate)
    signs_draw = jnp.clip(jax.random.normal(signs_key, (ORDER, G), jnp.float32), -4.0, 4.0)
    return (rate_value, signs_draw * jnp.sqrt(2.0 * rate_value / ORDER))


def draw_decay_rate(key, part):
    return filter_pair(key)[0]


def draw_residue(key, part):
    return filter_pair(key)[1]


def levels(stream_key, shape, cuts, least, top_value):
    loudness = 1.0
    for dim, blocks in cuts:
        draws = jax.random.uniform(jax.random.fold_in(jax.random.fold_in(stream_key, 6), dim), (blocks,), jnp.float32, least / len(cuts), top_value / len(cuts))
        loudness = loudness * jnp.repeat(jnp.exp(draws), shape[dim] // blocks).reshape((-1,) + (1,) * (len(shape) - 1 - dim))
    return loudness


def scatter_about(key, dims, scale, bound, pieces=(), kind=jnp.bfloat16):
    values = scale * jax.random.normal(key, dims, jnp.float32)
    if pieces:
        values = values * levels(key, dims, pieces, -0.22, 0.18)
    return jnp.clip(values, -bound, bound).astype(kind)


def setup_inputs(seed: int = 0) -> dict:
    arg_keys = jax.random.split(jax.random.key(seed), 5)
    stream = scatter_about(arg_keys[0], (3, TOKENS, D), 1.0, 6.0, ((1, 8), (2, 4)))
    short_taps = scatter_about(arg_keys[1], (3, TAPS, D), TAPS ** -0.5, 3.5, (), jnp.float32)
    decay_rate = draw_decay_rate(jax.random.fold_in(arg_keys[4], 71), 0)
    residue = draw_residue(jax.random.fold_in(arg_keys[4], 71), 0)
    return {"stream": stream, "short_taps": short_taps, "decay_rate": decay_rate, "residue": residue}


def unfold_taps(seq_taps):
    group_count, length = seq_taps.shape
    padded = jnp.concatenate([seq_taps, jnp.zeros((group_count, length + 1), seq_taps.dtype)], 1)
    tiled = jnp.tile(padded, (1, length))[:, : 2 * length * length]
    return tiled.reshape(group_count, length, 2 * length)[:, :, :length]


def reference(stream, short_taps, decay_rate, residue):
    total = stream.shape[1]
    chan_count = stream.shape[2]
    group_count = chan_count // GROUP
    reach = short_taps.shape[1] - 1
    widened = jnp.pad(stream.astype(jnp.float32), ((0, 0), (reach, 0), (0, 0)))
    features = short_taps[:, 0, None, :] * widened[:, reach:, :]
    for lag in range(1, reach + 1):
        features = features + short_taps[:, lag, None, :] * widened[:, reach - lag: reach - lag + total, :]
    query = features[0]
    product = features[1] * features[2]
    block = math.gcd(total, 128)
    position = jnp.arange(block, dtype=jnp.float32)
    powers = jnp.exp(-decay_rate[:, :, None] * position)
    seq_taps = jnp.sum(residue[:, :, None] * powers, 0)
    toeplitz = unfold_taps(seq_taps)
    closing = jnp.exp(-decay_rate[:, :, None] * (block - 1.0 - position))
    opening = residue[:, :, None] * jnp.exp(-decay_rate[:, :, None] * (position + 1.0))
    span_decay = jnp.exp(-decay_rate * block)
    blocks = product.reshape(total // block, block, group_count, GROUP)

    def advance(state, piece):
        local_part = jnp.einsum('gst,sgc->tgc', toeplitz, piece, precision=lax.Precision.HIGHEST)
        tail_part = jnp.einsum('rgt,rgc->tgc', opening, state, precision=lax.Precision.HIGHEST)
        fresh = jnp.einsum('rgs,sgc->rgc', closing, piece, precision=lax.Precision.HIGHEST)
        return span_decay[:, :, None] * state + fresh, local_part + tail_part

    start_state = jnp.zeros((ORDER, group_count, GROUP), jnp.float32)
    final_state, convolved = lax.scan(advance, start_state, blocks)
    convolved = convolved.reshape(total, chan_count)
    return (query * convolved).astype(jnp.bfloat16)
```

```python
import functools

import jax
import jax.numpy as jnp
from jax import lax
from jax.experimental import pallas as pl
from jax.experimental.pallas import tpu as pltpu
from jax.sharding import PartitionSpec as P

GROUP = 16
LANES = 128
CHUNKS = 2
DICT = pl.DeviceIdType.MESH


def kernel(
    n_ctx, n_dp,
    stream, taps, rate, resid, out,
    xv, tp, rates, resids, hs, hr, x0, prod, query, conv, sel, dec, amp, span, end, end_in,
    chain_in, other_in, chain_out, zs,
    local_sem, dp_send, dp_recv, halo_sem, end_send, end_recv, chain_send, chain_recv, fwd_send, fwd_recv,
):
    k = lax.axis_index("ctx")
    dp = lax.axis_index("dp")
    core = lax.rem(k, 2)
    z = k // 2
    last_z = n_ctx // 2 - 1
    partner = k + 1 - 2 * core
    T, C = stream.shape[1], stream.shape[2]
    J = C // LANES
    HJ = J // 2
    reach = taps.shape[1] - 1
    own_poles, G = rate.shape
    R = own_poles * n_dp
    RC = R // CHUNKS
    blocks = T // 16
    f32 = jnp.float32

    loads = []
    for n, i in enumerate((1, 2, 0)):
        loads.append(pltpu.make_async_copy(stream.at[i], xv.at[i], local_sem.at[n]))
    loads.append(pltpu.make_async_copy(taps.at[:, :, pl.ds(pl.multiple_of(dp * C, LANES), C)], tp, local_sem.at[3]))
    own_rate = pltpu.make_async_copy(rate, rates.at[dp], local_sem.at[4])
    own_resid = pltpu.make_async_copy(resid, resids.at[dp], local_sem.at[5])
    for c in loads:
        c.start()
    own_rate.start()
    own_resid.start()

    barrier = pltpu.get_barrier_semaphore()

    def greet(**where):
        pl.semaphore_signal(barrier, inc=1, device_id=where, device_id_type=DICT)

    for d in range(1, n_dp):
        greet(dp=lax.rem(dp + d, n_dp))
    greet(ctx=partner)
    beside = k - 1 + 2 * core
    has_beside = jnp.logical_and(beside >= 0, beside < n_ctx)
    has_prev, has_next = z > 0, z < last_z

    @pl.when(has_beside)
    def _():
        greet(ctx=beside)

    @pl.when(has_prev)
    def _():
        greet(ctx=k - 2)

    @pl.when(has_next)
    def _():
        greet(ctx=k + 2)

    pl.semaphore_wait(
        barrier,
        n_dp + has_beside.astype(jnp.int32) + has_prev.astype(jnp.int32) + has_next.astype(jnp.int32),
    )

    def dp_copy(which, d, owner, peer):
        src, dst = ((rate, rates), (resid, resids))[which]
        return pltpu.make_async_remote_copy(
            src_ref=src, dst_ref=dst.at[owner], send_sem=dp_send.at[which, d - 1],
            recv_sem=dp_recv.at[which, d - 1], device_id={"dp": peer}, device_id_type=DICT)

    for d in range(1, n_dp):
        for which in range(2):
            dp_copy(which, d, dp, lax.rem(dp + d, n_dp)).start()

    for c in loads:
        c.wait()
    for i in range(3):
        hs[i] = xv[i, T - 16:T, :].astype(f32)[16 - reach:16]

    def halo():
        return pltpu.make_async_remote_copy(
            src_ref=hs, dst_ref=hr, send_sem=halo_sem.at[0], recv_sem=halo_sem.at[1],
            device_id={"ctx": k + 1}, device_id_type=DICT)

    @pl.when(k < n_ctx - 1)
    def _():
        halo().start()

    def feature(i, j, window):
        cols = pl.ds(j * LANES, LANES)
        total = tp[i, 0:1, cols] * window[8:24]
        for lag in range(1, reach + 1):
            total = total + tp[i, lag:lag + 1, cols] * window[8 - lag:24 - lag]
        return total

    def window_at(i, j, b):
        cols = pl.ds(j * LANES, LANES)
        before = xv[i, pl.ds(pl.multiple_of(b * 16 - 16, 16), 16), cols].astype(f32)
        here = xv[i, pl.ds(pl.multiple_of(b * 16, 16), 16), cols].astype(f32)
        return jnp.concatenate([before[8:16], here], 0)

    def window_first(i, j):
        return x0[i, :, pl.ds(j * LANES, LANES)]

    def put(ref, b, j, tile):
        for u in range(2):
            ref[pl.ds(pl.multiple_of(((2 * b + u) * J + j) * 8, 8), 8), :] = tile[8 * u:8 * u + 8]

    @pl.loop(1, blocks)
    def _(b):
        for j in range(J):
            put(prod, b, j, feature(1, j, window_at(1, j, b)) * feature(2, j, window_at(2, j, b)))

    own_rate.wait()
    own_resid.wait()
    for d in range(1, n_dp):
        for which in range(2):
            dp_copy(which, d, lax.rem(dp + n_dp - d, n_dp), dp).wait_recv()

    per_tile = LANES // GROUP
    tile_of = lax.broadcasted_iota(jnp.int32, (HJ, G), 1) // per_tile
    row = lax.broadcasted_iota(jnp.int32, (HJ, G), 0)
    spread = (
        lax.rem(lax.broadcasted_iota(jnp.int32, (G, LANES), 0), per_tile)
        == lax.broadcasted_iota(jnp.int32, (G, LANES), 1) // GROUP
    ).astype(f32)
    for source, is_rate in ((rates, True), (resids, False)):
        for h in range(2):
            mask = tile_of == dp * J + h * HJ + row
            for r in range(R):
                line = source[r // own_poles, r % own_poles:r % own_poles + 1, :]
                sel[(h * R + r) * HJ:(h * R + r + 1) * HJ, :] = jnp.where(mask, line, 0.0)
        wide = jnp.dot(sel[...], spread, precision=lax.Precision.HIGHEST, preferred_element_type=f32)
        for h in range(2):
            for r in range(R):
                part = wide[(h * R + r) * HJ:(h * R + r + 1) * HJ]
                if is_rate:
                    dec[h, r] = jnp.exp(-part)
                    span[h, r] = jnp.exp(-part * T)
                else:
                    amp[h, r] = part

    @pl.when(k == 0)
    def _():
        hr[...] = jnp.zeros_like(hr)

    @pl.when(k > 0)
    def _():
        halo().wait_recv()

    for i in range(3):
        x0[i, 8 - reach:8, :] = hr[i]
        x0[i, 8:24, :] = xv[i, 0:16, :].astype(f32)
    for j in range(J):
        put(prod, 0, j, feature(1, j, window_first(1, j)) * feature(2, j, window_first(2, j)))

    def rows(tb, h, u):
        return pl.ds(tb * (J * 8) + h * (HJ * 8) + u, HJ, stride=8)

    def close(h):
        decay = [dec[h, r] for r in range(R)]

        def body(tb, state):
            for u in range(8):
                x = prod[rows(tb, h, u), :]
                state = tuple(a * s + x for a, s in zip(decay, state))
            return state

        state = lax.fori_loop(0, T // 8, body, tuple(jnp.zeros((HJ, LANES), f32) for _ in range(R)))
        for r in range(R):
            end[h, r] = state[r]

    def end_copy(h):
        return pltpu.make_async_remote_copy(
            src_ref=end.at[h], dst_ref=end_in.at[h], send_sem=end_send.at[h], recv_sem=end_recv.at[h],
            device_id={"ctx": partner}, device_id_type=DICT)

    close(1 - core)
    end_copy(1 - core).start()
    close(core)

    @pl.when(core == 0)
    def _():
        end_copy(0).start()

    def total_of_chip():
        end_copy(core).wait_recv()
        for r in range(R):
            own, other = end[core, r], end_in[core, r]
            first = jnp.where(core == 0, own, other)
            second = jnp.where(core == 0, other, own)
            chain_out[r // RC, r % RC] = span[core, r] * first + second

    def chain_copy(c):
        return pltpu.make_async_remote_copy(
            src_ref=chain_out.at[c], dst_ref=chain_in.at[c], send_sem=chain_send.at[c],
            recv_sem=chain_recv.at[c], device_id={"ctx": k + 2}, device_id_type=DICT)

    def forward(c):
        return pltpu.make_async_remote_copy(
            src_ref=chain_in.at[c], dst_ref=other_in.at[c], send_sem=fwd_send.at[c],
            recv_sem=fwd_recv.at[c], device_id={"ctx": partner}, device_id_type=DICT)

    def relay():
        for c in range(CHUNKS):
            chain_copy(c).wait_recv()

            @pl.when(has_next)
            def _():
                for q in range(RC):
                    leap = span[core, c * RC + q]
                    chain_out[c, q] = chain_out[c, q] + leap * leap * chain_in[c, q]
                chain_copy(c).start()

            forward(c).start()

    total_of_chip()

    @pl.when(z == 0)
    def _():
        for c in range(CHUNKS):
            @pl.when(has_next)
            def _():
                chain_copy(c).start()
        chain_in[...] = jnp.zeros_like(chain_in)
        other_in[...] = jnp.zeros_like(other_in)

    for j in range(J):
        put(query, 0, j, feature(0, j, window_first(0, j)))

    @pl.loop(1, blocks)
    def _(b):
        for j in range(J):
            put(query, b, j, feature(0, j, window_at(0, j, b)))

    def inside(h):
        decay = [dec[h, r] for r in range(R)]
        gain = [amp[h, r] for r in range(R)]

        def body(tb, state):
            for u in range(8):
                x = prod[rows(tb, h, u), :]
                state = tuple(a * s + x for a, s in zip(decay, state))
                terms = [g * s for g, s in zip(gain, state)]
                while len(terms) > 1:
                    terms = [sum(terms[n:n + 2][1:], terms[n]) for n in range(0, len(terms), 2)]
                conv[rows(tb, h, u), :] = terms[0]
            return state

        lax.fori_loop(0, T // 8, body, tuple(jnp.zeros((HJ, LANES), f32) for _ in range(R)))

    inside(0)

    @pl.when(z == 1)
    def _():
        relay()

    inside(1)

    @pl.when(z > 1)
    def _():
        relay()

    @pl.when(core == 1)
    def _():
        end_copy(0).wait_recv()

    def tail(h, source):
        for r in range(R):
            zs[r] = source[r // RC, r % RC]

        @pl.when(core == 1)
        def _():
            for r in range(R):
                zs[r] = span[h, r] * zs[r] + end_in[h, r]

        decay = [dec[h, r] for r in range(R)]

        def body(tb, state):
            for u in range(8):
                state = tuple(a * s for a, s in zip(decay, state))
                terms = list(state)
                while len(terms) > 1:
                    terms = [sum(terms[n:n + 2][1:], terms[n]) for n in range(0, len(terms), 2)]
                conv[rows(tb, h, u), :] = conv[rows(tb, h, u), :] + terms[0]
            return state

        lax.fori_loop(0, T // 8, body, tuple(amp[h, r] * zs[r] for r in range(R)))

    tail(core, chain_in)

    @pl.when(has_prev)
    def _():
        for c in range(CHUNKS):
            forward(c).wait_recv()

    tail(1 - core, other_in)

    @pl.loop(0, blocks)
    def _(b):
        for j in range(J):
            tiles = []
            for u in range(2):
                at = pl.ds(pl.multiple_of(((2 * b + u) * J + j) * 8, 8), 8)
                tiles.append(query[at, :] * conv[at, :])
            out[pl.ds(pl.multiple_of(b * 16, 16), 16), pl.ds(j * LANES, LANES)] = jnp.concatenate(
                tiles, 0).astype(out.dtype)

    for d in range(1, n_dp):
        for which in range(2):
            dp_copy(which, d, dp, lax.rem(dp + d, n_dp)).wait_send()

    @pl.when(k < n_ctx - 1)
    def _():
        halo().wait_send()

    end_copy(1 - core).wait_send()

    @pl.when(core == 0)
    def _():
        end_copy(0).wait_send()

    for c in range(CHUNKS):
        @pl.when(has_next)
        def _():
            chain_copy(c).wait_send()

        @pl.when(has_prev)
        def _():
            forward(c).wait_send()


def solution(mesh):
    n_ctx, n_dp = mesh.shape["ctx"], mesh.shape["dp"]

    def shards(stream, short_taps, decay_rate, residue):
        T, C = stream.shape[1], stream.shape[2]
        n_taps = short_taps.shape[1]
        own_poles, G = decay_rate.shape
        R = own_poles * n_dp
        HJ = C // LANES // 2
        RC = R // CHUNKS
        f32 = jnp.float32
        dma = pltpu.SemaphoreType.DMA
        flat = pltpu.VMEM((T * C // LANES, LANES), f32)
        halves = pltpu.VMEM((2, R, HJ, LANES), f32)
        piece = pltpu.VMEM((CHUNKS, RC, HJ, LANES), f32)
        edge = pltpu.VMEM((3, n_taps - 1, C), f32)
        return pl.pallas_call(
            functools.partial(kernel, n_ctx, n_dp),
            out_shape=jax.ShapeDtypeStruct((T, C), jnp.bfloat16),
            in_specs=[pl.BlockSpec(memory_space=pl.ANY)] * 4,
            out_specs=pl.BlockSpec(memory_space=pltpu.VMEM),
            scratch_shapes=[
                pltpu.VMEM((3, T, C), jnp.bfloat16),
                pltpu.VMEM((3, n_taps, C), f32),
                pltpu.VMEM((n_dp, own_poles, G), f32),
                pltpu.VMEM((n_dp, own_poles, G), f32),
                edge, edge,
                pltpu.VMEM((3, 24, C), f32),
                flat, flat, flat,
                pltpu.VMEM((2 * R * HJ, G), f32),
                halves, halves, halves, halves, halves,
                piece, piece, piece,
                pltpu.VMEM((R, HJ, LANES), f32),
                dma((6,)),
                dma((2, n_dp - 1)), dma((2, n_dp - 1)),
                dma((2,)),
                dma((2,)), dma((2,)),
                dma((CHUNKS,)), dma((CHUNKS,)),
                dma((CHUNKS,)), dma((CHUNKS,)),
            ],
            compiler_params=pltpu.CompilerParams(
                collective_id=0, has_side_effects=True, vmem_limit_bytes=32 * 1024 * 1024),
            cost_estimate=pl.CostEstimate(
                flops=8 * R * T * C, bytes_accessed=8 * T * C, transcendentals=0),
        )(stream, short_taps, decay_rate, residue)

    in_specs = (P(None, "ctx", "dp"), P(), P("dp", None), P("dp", None))
    return jax.shard_map(shards, mesh=mesh, in_specs=in_specs, out_specs=P("ctx", "dp"), check_vma=False)
```

```python
import functools

import jax
import jax.numpy as jnp
from jax import lax
from jax.experimental import pallas as pl
from jax.experimental.pallas import tpu as pltpu
from jax.sharding import PartitionSpec as P

GROUP = 16
LANES = 128
CHUNKS = 4
PARTS = 2
DICT = pl.DeviceIdType.MESH


def kernel(
    n_ctx, n_dp,
    stream, taps, rate, resid, out,
    xv, tp, rates, resids, hs, hr, x0, prod, query, conv, sel, dec, amp, span, end, end_in,
    chain_in, other_in, chain_out, zs,
    local_sem, dp_send, dp_recv, halo_sem, end_send, end_recv, chain_send, chain_recv, fwd_send, fwd_recv,
):
    k = lax.axis_index("ctx")
    dp = lax.axis_index("dp")
    core = lax.rem(k, 2)
    z = k // 2
    last_z = n_ctx // 2 - 1
    partner = k + 1 - 2 * core
    T, C = stream.shape[1], stream.shape[2]
    J = C // LANES
    HJ = J // 2
    reach = taps.shape[1] - 1
    own_poles, G = rate.shape
    R = own_poles * n_dp
    RC = R // CHUNKS
    blocks = T // 16
    f32 = jnp.float32

    loads = []
    for n, i in enumerate((1, 2, 0)):
        loads.append(pltpu.make_async_copy(stream.at[i], xv.at[i], local_sem.at[n]))
    loads.append(pltpu.make_async_copy(taps.at[:, :, pl.ds(pl.multiple_of(dp * C, LANES), C)], tp, local_sem.at[3]))
    own_rate = pltpu.make_async_copy(rate, rates.at[dp], local_sem.at[4])
    own_resid = pltpu.make_async_copy(resid, resids.at[dp], local_sem.at[5])
    for c in loads:
        c.start()
    own_rate.start()
    own_resid.start()

    barrier = pltpu.get_barrier_semaphore()

    def greet(**where):
        pl.semaphore_signal(barrier, inc=1, device_id=where, device_id_type=DICT)

    for d in range(1, n_dp):
        greet(dp=lax.rem(dp + d, n_dp))
    greet(ctx=partner)
    beside = k - 1 + 2 * core
    has_beside = jnp.logical_and(beside >= 0, beside < n_ctx)
    has_prev, has_next = z > 0, z < last_z

    @pl.when(has_beside)
    def _():
        greet(ctx=beside)

    @pl.when(has_prev)
    def _():
        greet(ctx=k - 2)

    @pl.when(has_next)
    def _():
        greet(ctx=k + 2)

    pl.semaphore_wait(
        barrier,
        n_dp + has_beside.astype(jnp.int32) + has_prev.astype(jnp.int32) + has_next.astype(jnp.int32),
    )

    def dp_copy(which, d, owner, peer):
        src, dst = ((rate, rates), (resid, resids))[which]
        return pltpu.make_async_remote_copy(
            src_ref=src, dst_ref=dst.at[owner], send_sem=dp_send.at[which, d - 1],
            recv_sem=dp_recv.at[which, d - 1], device_id={"dp": peer}, device_id_type=DICT)

    for which in range(2):
        for d in range(1, n_dp):
            dp_copy(which, d, dp, lax.rem(dp + d, n_dp)).start()

    for c in loads:
        c.wait()
    for i in range(3):
        hs[i] = xv[i, T - 16:T, :].astype(f32)[16 - reach:16]

    def halo():
        return pltpu.make_async_remote_copy(
            src_ref=hs, dst_ref=hr, send_sem=halo_sem.at[0], recv_sem=halo_sem.at[1],
            device_id={"ctx": k + 1}, device_id_type=DICT)

    @pl.when(k < n_ctx - 1)
    def _():
        halo().start()

    def feature(i, j, window):
        cols = pl.ds(j * LANES, LANES)
        total = tp[i, 0:1, cols] * window[8:24]
        for lag in range(1, reach + 1):
            total = total + tp[i, lag:lag + 1, cols] * window[8 - lag:24 - lag]
        return total

    def window_at(i, j, b):
        cols = pl.ds(j * LANES, LANES)
        before = xv[i, pl.ds(pl.multiple_of(b * 16 - 16, 16), 16), cols].astype(f32)
        here = xv[i, pl.ds(pl.multiple_of(b * 16, 16), 16), cols].astype(f32)
        return jnp.concatenate([before[8:16], here], 0)

    def window_first(i, j):
        return x0[i, :, pl.ds(j * LANES, LANES)]

    def put(ref, b, j, tile):
        for u in range(2):
            ref[pl.ds(pl.multiple_of(((2 * b + u) * J + j) * 8, 8), 8), :] = tile[8 * u:8 * u + 8]

    @pl.loop(1, blocks)
    def _(b):
        for j in range(J):
            put(prod, b, j, feature(1, j, window_at(1, j, b)) * feature(2, j, window_at(2, j, b)))

    own_rate.wait()
    for d in range(1, n_dp):
        dp_copy(0, d, lax.rem(dp + n_dp - d, n_dp), dp).wait_recv()

    per_tile = LANES // GROUP
    groups = C // GROUP
    width = sel.shape[1]
    base = dp * groups
    window_start = base // width * width
    tile_of = (lax.broadcasted_iota(jnp.int32, (HJ, width), 1) - (base - window_start)) // per_tile
    row = lax.broadcasted_iota(jnp.int32, (HJ, width), 0)
    spread = (
        lax.rem(lax.broadcasted_iota(jnp.int32, (width, LANES), 0), per_tile)
        == lax.broadcasted_iota(jnp.int32, (width, LANES), 1) // GROUP
    ).astype(f32)
    shown = pl.ds(pl.multiple_of(window_start, LANES), width)

    def widen(source, use):
        for h in range(2):
            mask = tile_of == h * HJ + row
            for r in range(R):
                line = source[r // own_poles, r % own_poles:r % own_poles + 1, shown]
                sel[(h * R + r) * HJ:(h * R + r + 1) * HJ, :] = jnp.where(mask, line, 0.0)
        wide = jnp.dot(sel[...], spread, precision=lax.Precision.HIGHEST, preferred_element_type=f32)
        for h in range(2):
            for r in range(R):
                use(h, r, wide[(h * R + r) * HJ:(h * R + r + 1) * HJ])

    def use_rate(h, r, part):
        dec[h, r] = jnp.exp(-part)
        span[h, r] = jnp.exp(-part * T)

    def use_resid(h, r, part):
        amp[h, r] = part

    widen(rates, use_rate)

    @pl.when(k == 0)
    def _():
        hr[...] = jnp.zeros_like(hr)

    @pl.when(k > 0)
    def _():
        halo().wait_recv()

    for i in range(3):
        x0[i, 8 - reach:8, :] = hr[i]
        x0[i, 8:24, :] = xv[i, 0:16, :].astype(f32)
    for j in range(J):
        put(prod, 0, j, feature(1, j, window_first(1, j)) * feature(2, j, window_first(2, j)))

    def rows(tb, h, u):
        return pl.ds(tb * (J * 8) + h * (HJ * 8) + u, HJ, stride=8)

    RP = R // PARTS

    def close(part):
        slots = [(h, r) for h in range(2) for r in range(part * RP, (part + 1) * RP)]
        decay = [dec[h, r] for h, r in slots]

        def body(tb, state):
            for u in range(8):
                x = [prod[rows(tb, h, u), :] for h in range(2)]
                state = tuple(a * s + x[slot[0]] for slot, a, s in zip(slots, decay, state))
            return state

        state = lax.fori_loop(0, T // 8, body, tuple(jnp.zeros((HJ, LANES), f32) for _ in slots))
        for (h, r), value in zip(slots, state):
            end[h, r] = value

    def end_copy(h, part):
        piece = pl.ds(part * RP, RP)
        return pltpu.make_async_remote_copy(
            src_ref=end.at[h, piece], dst_ref=end_in.at[h, piece], send_sem=end_send.at[h, part],
            recv_sem=end_recv.at[h, part], device_id={"ctx": partner}, device_id_type=DICT)

    for part in range(PARTS):
        close(part)
        end_copy(1 - core, part).start()

    @pl.when(core == 0)
    def _():
        for part in range(PARTS):
            end_copy(0, part).start()

    def total_of_chip(part):
        end_copy(core, part).wait_recv()
        for r in range(part * RP, (part + 1) * RP):
            own, other = end[core, r], end_in[core, r]
            first = jnp.where(core == 0, own, other)
            second = jnp.where(core == 0, other, own)
            chain_out[r // RC, r % RC] = span[core, r] * first + second

    def chain_copy(c):
        return pltpu.make_async_remote_copy(
            src_ref=chain_out.at[c], dst_ref=chain_in.at[c], send_sem=chain_send.at[c],
            recv_sem=chain_recv.at[c], device_id={"ctx": k + 2}, device_id_type=DICT)

    def forward(c):
        return pltpu.make_async_remote_copy(
            src_ref=chain_in.at[c], dst_ref=other_in.at[c], send_sem=fwd_send.at[c],
            recv_sem=fwd_recv.at[c], device_id={"ctx": partner}, device_id_type=DICT)

    def relay():
        for c in range(CHUNKS):
            chain_copy(c).wait_recv()

            @pl.when(has_next)
            def _():
                for q in range(RC):
                    leap = span[core, c * RC + q]
                    chain_out[c, q] = chain_out[c, q] + leap * leap * chain_in[c, q]
                chain_copy(c).start()

            forward(c).start()

    for part in range(PARTS):
        total_of_chip(part)

        @pl.when(jnp.logical_and(z == 0, has_next))
        def _():
            for c in range(part * RP // RC, (part + 1) * RP // RC):
                chain_copy(c).start()

    @pl.when(z == 0)
    def _():
        chain_in[...] = jnp.zeros_like(chain_in)
        other_in[...] = jnp.zeros_like(other_in)

    own_resid.wait()
    for d in range(1, n_dp):
        dp_copy(1, d, lax.rem(dp + n_dp - d, n_dp), dp).wait_recv()
    widen(resids, use_resid)

    for j in range(J):
        put(query, 0, j, feature(0, j, window_first(0, j)))

    @pl.loop(1, blocks)
    def _(b):
        for j in range(J):
            put(query, b, j, feature(0, j, window_at(0, j, b)))

    def inside(h):
        decay = [dec[h, r] for r in range(R)]
        gain = [amp[h, r] for r in range(R)]

        def body(tb, state):
            for u in range(8):
                x = prod[rows(tb, h, u), :]
                state = tuple(a * s + x for a, s in zip(decay, state))
                terms = [g * s for g, s in zip(gain, state)]
                while len(terms) > 1:
                    terms = [sum(terms[n:n + 2][1:], terms[n]) for n in range(0, len(terms), 2)]
                conv[rows(tb, h, u), :] = terms[0]
            return state

        lax.fori_loop(0, T // 8, body, tuple(jnp.zeros((HJ, LANES), f32) for _ in range(R)))

    @pl.when(z == 1)
    def _():
        relay()

    inside(0)

    @pl.when(z == 2)
    def _():
        relay()

    inside(1)

    @pl.when(z > 2)
    def _():
        relay()

    @pl.when(core == 1)
    def _():
        for part in range(PARTS):
            end_copy(0, part).wait_recv()

    def tail(h, source):
        for r in range(R):
            zs[r] = source[r // RC, r % RC]

        @pl.when(core == 1)
        def _():
            for r in range(R):
                zs[r] = span[h, r] * zs[r] + end_in[h, r]

        decay = [dec[h, r] for r in range(R)]

        def body(tb, state):
            for u in range(8):
                state = tuple(a * s for a, s in zip(decay, state))
                terms = list(state)
                while len(terms) > 1:
                    terms = [sum(terms[n:n + 2][1:], terms[n]) for n in range(0, len(terms), 2)]
                conv[rows(tb, h, u), :] = conv[rows(tb, h, u), :] + terms[0]
            return state

        lax.fori_loop(0, T // 8, body, tuple(amp[h, r] * zs[r] for r in range(R)))

    def gate(h):
        @pl.loop(0, blocks)
        def _(b):
            for j in range(HJ):
                tiles = []
                for u in range(2):
                    at = pl.ds(pl.multiple_of(((2 * b + u) * J + h * HJ + j) * 8, 8), 8)
                    tiles.append(query[at, :] * conv[at, :])
                cols = pl.ds(pl.multiple_of((h * HJ + j) * LANES, LANES), LANES)
                out[pl.ds(pl.multiple_of(b * 16, 16), 16), cols] = jnp.concatenate(tiles, 0).astype(out.dtype)

    tail(core, chain_in)
    gate(core)

    @pl.when(has_prev)
    def _():
        for c in range(CHUNKS):
            forward(c).wait_recv()

    tail(1 - core, other_in)
    gate(1 - core)

    for d in range(1, n_dp):
        for which in range(2):
            dp_copy(which, d, dp, lax.rem(dp + d, n_dp)).wait_send()

    @pl.when(k < n_ctx - 1)
    def _():
        halo().wait_send()

    for part in range(PARTS):
        end_copy(1 - core, part).wait_send()

    @pl.when(core == 0)
    def _():
        for part in range(PARTS):
            end_copy(0, part).wait_send()

    for c in range(CHUNKS):
        @pl.when(has_next)
        def _():
            chain_copy(c).wait_send()

        @pl.when(has_prev)
        def _():
            forward(c).wait_send()


def solution(mesh):
    n_ctx, n_dp = mesh.shape["ctx"], mesh.shape["dp"]

    def shards(stream, short_taps, decay_rate, residue):
        T, C = stream.shape[1], stream.shape[2]
        n_taps = short_taps.shape[1]
        own_poles, G = decay_rate.shape
        R = own_poles * n_dp
        HJ = C // LANES // 2
        RC = R // CHUNKS
        f32 = jnp.float32
        dma = pltpu.SemaphoreType.DMA
        flat = pltpu.VMEM((T * C // LANES, LANES), f32)
        halves = pltpu.VMEM((2, R, HJ, LANES), f32)
        piece = pltpu.VMEM((CHUNKS, RC, HJ, LANES), f32)
        edge = pltpu.VMEM((3, n_taps - 1, C), f32)
        return pl.pallas_call(
            functools.partial(kernel, n_ctx, n_dp),
            out_shape=jax.ShapeDtypeStruct((T, C), jnp.bfloat16),
            in_specs=[pl.BlockSpec(memory_space=pl.ANY)] * 4,
            out_specs=pl.BlockSpec(memory_space=pltpu.VMEM),
            scratch_shapes=[
                pltpu.VMEM((3, T, C), jnp.bfloat16),
                pltpu.VMEM((3, n_taps, C), f32),
                pltpu.VMEM((n_dp, own_poles, G), f32),
                pltpu.VMEM((n_dp, own_poles, G), f32),
                edge, edge,
                pltpu.VMEM((3, 24, C), f32),
                flat, flat, flat,
                pltpu.VMEM((2 * R * HJ, max(C // GROUP, LANES)), f32),
                halves, halves, halves, halves, halves,
                piece, piece, piece,
                pltpu.VMEM((R, HJ, LANES), f32),
                dma((6,)),
                dma((2, n_dp - 1)), dma((2, n_dp - 1)),
                dma((2,)),
                dma((2, PARTS)), dma((2, PARTS)),
                dma((CHUNKS,)), dma((CHUNKS,)),
                dma((CHUNKS,)), dma((CHUNKS,)),
            ],
            compiler_params=pltpu.CompilerParams(
                collective_id=0, has_side_effects=True, vmem_limit_bytes=60 * 1024 * 1024),
            cost_estimate=pl.CostEstimate(
                flops=8 * R * T * C, bytes_accessed=8 * T * C, transcendentals=0),
        )(stream, short_taps, decay_rate, residue)

    in_specs = (P(None, "ctx", "dp"), P(), P("dp", None), P("dp", None))
    return jax.shard_map(shards, mesh=mesh, in_specs=in_specs, out_specs=P("ctx", "dp"), check_vma=False)
```

```python
import functools

import jax
import jax.numpy as jnp
from jax import lax
from jax.experimental import pallas as pl
from jax.experimental.pallas import tpu as pltpu
from jax.sharding import PartitionSpec as P

GROUP = 16
LANES = 128
CHUNKS = 4
PARTS = 2
DICT = pl.DeviceIdType.MESH


def kernel(
    n_ctx, n_dp,
    stream, taps, rate, resid, out,
    xv, tp, rates, resids, hs, hr, x0, prod, query, conv, sel, dec, amp, span, end, end_in,
    chain_in, other_in, chain_out, zs,
    local_sem, dp_send, dp_recv, halo_sem, end_send, end_recv, chain_send, chain_recv, fwd_send, fwd_recv,
):
    k = lax.axis_index("ctx")
    dp = lax.axis_index("dp")
    core = lax.rem(k, 2)
    z = k // 2
    last_z = n_ctx // 2 - 1
    partner = k + 1 - 2 * core
    T, C = stream.shape[1], stream.shape[2]
    J = C // LANES
    HJ = J // 2
    reach = taps.shape[1] - 1
    own_poles, G = rate.shape
    R = own_poles * n_dp
    RC = R // CHUNKS
    blocks = T // 16
    f32 = jnp.float32

    loads = []
    for n, i in enumerate((1, 2, 0)):
        loads.append(pltpu.make_async_copy(stream.at[i], xv.at[i], local_sem.at[n]))
    loads.append(pltpu.make_async_copy(taps.at[:, :, pl.ds(pl.multiple_of(dp * C, LANES), C)], tp, local_sem.at[3]))
    own_rate = pltpu.make_async_copy(rate, rates.at[dp], local_sem.at[4])
    own_resid = pltpu.make_async_copy(resid, resids.at[dp], local_sem.at[5])
    for c in loads:
        c.start()
    own_rate.start()
    own_resid.start()

    barrier = pltpu.get_barrier_semaphore()

    def greet(**where):
        pl.semaphore_signal(barrier, inc=1, device_id=where, device_id_type=DICT)

    for d in range(1, n_dp):
        greet(dp=lax.rem(dp + d, n_dp))
    greet(ctx=partner)
    beside = k - 1 + 2 * core
    has_beside = jnp.logical_and(beside >= 0, beside < n_ctx)
    has_prev, has_next = z > 0, z < last_z

    @pl.when(has_beside)
    def _():
        greet(ctx=beside)

    @pl.when(has_prev)
    def _():
        greet(ctx=k - 2)

    @pl.when(has_next)
    def _():
        greet(ctx=k + 2)

    pl.semaphore_wait(
        barrier,
        n_dp + has_beside.astype(jnp.int32) + has_prev.astype(jnp.int32) + has_next.astype(jnp.int32),
    )

    def dp_copy(which, d, owner, peer):
        src, dst = ((rate, rates), (resid, resids))[which]
        return pltpu.make_async_remote_copy(
            src_ref=src, dst_ref=dst.at[owner], send_sem=dp_send.at[which, d - 1],
            recv_sem=dp_recv.at[which, d - 1], device_id={"dp": peer}, device_id_type=DICT)

    for which in range(2):
        for d in range(1, n_dp):
            dp_copy(which, d, dp, lax.rem(dp + d, n_dp)).start()

    for c in loads:
        c.wait()
    for i in range(3):
        hs[i] = xv[i, T - 16:T, :].astype(f32)[16 - reach:16]

    def halo():
        return pltpu.make_async_remote_copy(
            src_ref=hs, dst_ref=hr, send_sem=halo_sem.at[0], recv_sem=halo_sem.at[1],
            device_id={"ctx": k + 1}, device_id_type=DICT)

    @pl.when(k < n_ctx - 1)
    def _():
        halo().start()

    def feature(i, j, window):
        cols = pl.ds(j * LANES, LANES)
        total = tp[i, 0:1, cols] * window[8:24]
        for lag in range(1, reach + 1):
            total = total + tp[i, lag:lag + 1, cols] * window[8 - lag:24 - lag]
        return total

    def window_at(i, j, b):
        cols = pl.ds(j * LANES, LANES)
        before = xv[i, pl.ds(pl.multiple_of(b * 16 - 16, 16), 16), cols].astype(f32)
        here = xv[i, pl.ds(pl.multiple_of(b * 16, 16), 16), cols].astype(f32)
        return jnp.concatenate([before[8:16], here], 0)

    def window_first(i, j):
        return x0[i, :, pl.ds(j * LANES, LANES)]

    def put(ref, b, j, tile):
        for u in range(2):
            ref[pl.ds(pl.multiple_of(((2 * b + u) * J + j) * 8, 8), 8), :] = tile[8 * u:8 * u + 8]

    @pl.loop(1, blocks)
    def _(b):
        for j in range(J):
            put(prod, b, j, feature(1, j, window_at(1, j, b)) * feature(2, j, window_at(2, j, b)))

    own_rate.wait()
    for d in range(1, n_dp):
        dp_copy(0, d, lax.rem(dp + n_dp - d, n_dp), dp).wait_recv()

    per_tile = LANES // GROUP
    groups = C // GROUP
    width = sel.shape[1]
    base = dp * groups
    window_start = base // width * width
    tile_of = (lax.broadcasted_iota(jnp.int32, (HJ, width), 1) - (base - window_start)) // per_tile
    row = lax.broadcasted_iota(jnp.int32, (HJ, width), 0)
    spread = (
        lax.rem(lax.broadcasted_iota(jnp.int32, (width, LANES), 0), per_tile)
        == lax.broadcasted_iota(jnp.int32, (width, LANES), 1) // GROUP
    ).astype(f32)
    shown = pl.ds(pl.multiple_of(window_start, LANES), width)

    def widen(source, use):
        for h in range(2):
            mask = tile_of == h * HJ + row
            for r in range(R):
                line = source[r // own_poles, r % own_poles:r % own_poles + 1, shown]
                sel[(h * R + r) * HJ:(h * R + r + 1) * HJ, :] = jnp.where(mask, line, 0.0)
        wide = jnp.dot(sel[...], spread, precision=lax.Precision.HIGHEST, preferred_element_type=f32)
        for h in range(2):
            for r in range(R):
                use(h, r, wide[(h * R + r) * HJ:(h * R + r + 1) * HJ])

    def use_rate(h, r, part):
        dec[h, r] = jnp.exp(-part)
        span[h, r] = jnp.exp(-part * T)

    def use_resid(h, r, part):
        amp[h, r] = part

    widen(rates, use_rate)

    @pl.when(k == 0)
    def _():
        hr[...] = jnp.zeros_like(hr)

    @pl.when(k > 0)
    def _():
        halo().wait_recv()

    for i in range(3):
        x0[i, 8 - reach:8, :] = hr[i]
        x0[i, 8:24, :] = xv[i, 0:16, :].astype(f32)
    for j in range(J):
        put(prod, 0, j, feature(1, j, window_first(1, j)) * feature(2, j, window_first(2, j)))

    def rows(tb, h, u):
        return pl.ds(tb * (J * 8) + h * (HJ * 8) + u, HJ, stride=8)

    RP = R // PARTS

    def close(part):
        slots = [(h, r) for h in range(2) for r in range(part * RP, (part + 1) * RP)]
        decay = [dec[h, r] for h, r in slots]

        def body(tb, state):
            for u in range(8):
                x = [prod[rows(tb, h, u), :] for h in range(2)]
                state = tuple(a * s + x[slot[0]] for slot, a, s in zip(slots, decay, state))
            return state

        state = lax.fori_loop(0, T // 8, body, tuple(jnp.zeros((HJ, LANES), f32) for _ in slots))
        for (h, r), value in zip(slots, state):
            end[h, r] = value

    def end_copy(h, part):
        piece = pl.ds(part * RP, RP)
        return pltpu.make_async_remote_copy(
            src_ref=end.at[h, piece], dst_ref=end_in.at[h, piece], send_sem=end_send.at[h, part],
            recv_sem=end_recv.at[h, part], device_id={"ctx": partner}, device_id_type=DICT)

    for part in range(PARTS):
        close(part)
        end_copy(1 - core, part).start()

    @pl.when(core == 0)
    def _():
        for part in range(PARTS):
            end_copy(0, part).start()

    def total_of_chip(part):
        end_copy(core, part).wait_recv()
        for r in range(part * RP, (part + 1) * RP):
            own, other = end[core, r], end_in[core, r]
            first = jnp.where(core == 0, own, other)
            second = jnp.where(core == 0, other, own)
            chain_out[r // RC, r % RC] = span[core, r] * first + second

    def chain_copy(c):
        return pltpu.make_async_remote_copy(
            src_ref=chain_out.at[c], dst_ref=chain_in.at[c], send_sem=chain_send.at[c],
            recv_sem=chain_recv.at[c], device_id={"ctx": k + 2}, device_id_type=DICT)

    def forward(c):
        return pltpu.make_async_remote_copy(
            src_ref=chain_in.at[c], dst_ref=other_in.at[c], send_sem=fwd_send.at[c],
            recv_sem=fwd_recv.at[c], device_id={"ctx": partner}, device_id_type=DICT)

    def relay():
        for c in range(CHUNKS):
            chain_copy(c).wait_recv()

            @pl.when(has_next)
            def _():
                for q in range(RC):
                    leap = span[core, c * RC + q]
                    chain_out[c, q] = chain_out[c, q] + leap * leap * chain_in[c, q]
                chain_copy(c).start()

            forward(c).start()

    for part in range(PARTS):
        total_of_chip(part)

        @pl.when(jnp.logical_and(z == 0, has_next))
        def _():
            for c in range(part * RP // RC, (part + 1) * RP // RC):
                chain_copy(c).start()

    @pl.when(z == 0)
    def _():
        chain_in[...] = jnp.zeros_like(chain_in)
        other_in[...] = jnp.zeros_like(other_in)

    own_resid.wait()
    for d in range(1, n_dp):
        dp_copy(1, d, lax.rem(dp + n_dp - d, n_dp), dp).wait_recv()
    widen(resids, use_resid)

    for j in range(J):
        put(query, 0, j, feature(0, j, window_first(0, j)))

    @pl.loop(1, blocks)
    def _(b):
        for j in range(J):
            put(query, b, j, feature(0, j, window_at(0, j, b)))

    def inside(h):
        decay = [dec[h, r] for r in range(R)]
        gain = [amp[h, r] for r in range(R)]

        def body(tb, state):
            for u in range(8):
                x = prod[rows(tb, h, u), :]
                state = tuple(a * s + x for a, s in zip(decay, state))
                terms = [g * s for g, s in zip(gain, state)]
                while len(terms) > 1:
                    terms = [sum(terms[n:n + 2][1:], terms[n]) for n in range(0, len(terms), 2)]
                conv[rows(tb, h, u), :] = terms[0]
            return state

        lax.fori_loop(0, T // 8, body, tuple(jnp.zeros((HJ, LANES), f32) for _ in range(R)))

    @pl.when(z == 1)
    def _():
        relay()

    inside(0)

    @pl.when(z == 2)
    def _():
        relay()

    inside(1)

    @pl.when(z > 2)
    def _():
        relay()

    @pl.when(core == 1)
    def _():
        for part in range(PARTS):
            end_copy(0, part).wait_recv()

    def tail(h, source):
        for r in range(R):
            zs[r] = source[r // RC, r % RC]

        @pl.when(core == 1)
        def _():
            for r in range(R):
                zs[r] = span[h, r] * zs[r] + end_in[h, r]

        decay = [dec[h, r] for r in range(R)]

        def body(tb, state):
            for u in range(8):
                state = tuple(a * s for a, s in zip(decay, state))
                terms = list(state)
                while len(terms) > 1:
                    terms = [sum(terms[n:n + 2][1:], terms[n]) for n in range(0, len(terms), 2)]
                conv[rows(tb, h, u), :] = conv[rows(tb, h, u), :] + terms[0]
            return state

        lax.fori_loop(0, T // 8, body, tuple(amp[h, r] * zs[r] for r in range(R)))

    def gate(h):
        @pl.loop(0, blocks)
        def _(b):
            for j in range(HJ):
                tiles = []
                for u in range(2):
                    at = pl.ds(pl.multiple_of(((2 * b + u) * J + h * HJ + j) * 8, 8), 8)
                    tiles.append(query[at, :] * conv[at, :])
                cols = pl.ds(pl.multiple_of((h * HJ + j) * LANES, LANES), LANES)
                out[pl.ds(pl.multiple_of(b * 16, 16), 16), cols] = jnp.concatenate(tiles, 0).astype(out.dtype)

    tail(core, chain_in)
    gate(core)

    @pl.when(has_prev)
    def _():
        for c in range(CHUNKS):
            forward(c).wait_recv()

    tail(1 - core, other_in)
    gate(1 - core)

    for d in range(1, n_dp):
        for which in range(2):
            dp_copy(which, d, dp, lax.rem(dp + d, n_dp)).wait_send()

    @pl.when(k < n_ctx - 1)
    def _():
        halo().wait_send()

    for part in range(PARTS):
        end_copy(1 - core, part).wait_send()

    @pl.when(core == 0)
    def _():
        for part in range(PARTS):
            end_copy(0, part).wait_send()

    for c in range(CHUNKS):
        @pl.when(has_next)
        def _():
            chain_copy(c).wait_send()

        @pl.when(has_prev)
        def _():
            forward(c).wait_send()


def solution(mesh):
    n_ctx, n_dp = mesh.shape["ctx"], mesh.shape["dp"]

    def shards(stream, short_taps, decay_rate, residue):
        T, C = stream.shape[1], stream.shape[2]
        n_taps = short_taps.shape[1]
        own_poles, G = decay_rate.shape
        R = own_poles * n_dp
        HJ = C // LANES // 2
        RC = R // CHUNKS
        f32 = jnp.float32
        dma = pltpu.SemaphoreType.DMA
        flat = pltpu.VMEM((T * C // LANES, LANES), f32)
        halves = pltpu.VMEM((2, R, HJ, LANES), f32)
        piece = pltpu.VMEM((CHUNKS, RC, HJ, LANES), f32)
        edge = pltpu.VMEM((3, n_taps - 1, C), f32)
        return pl.pallas_call(
            functools.partial(kernel, n_ctx, n_dp),
            out_shape=pltpu.VMEM((T, C), jnp.bfloat16),
            in_specs=[pl.BlockSpec(memory_space=pl.ANY)] * 4,
            out_specs=pl.BlockSpec(memory_space=pltpu.VMEM),
            scratch_shapes=[
                pltpu.VMEM((3, T, C), jnp.bfloat16),
                pltpu.VMEM((3, n_taps, C), f32),
                pltpu.VMEM((n_dp, own_poles, G), f32),
                pltpu.VMEM((n_dp, own_poles, G), f32),
                edge, edge,
                pltpu.VMEM((3, 24, C), f32),
                flat, flat, flat,
                pltpu.VMEM((2 * R * HJ, max(C // GROUP, LANES)), f32),
                halves, halves, halves, halves, halves,
                piece, piece, piece,
                pltpu.VMEM((R, HJ, LANES), f32),
                dma((6,)),
                dma((2, n_dp - 1)), dma((2, n_dp - 1)),
                dma((2,)),
                dma((2, PARTS)), dma((2, PARTS)),
                dma((CHUNKS,)), dma((CHUNKS,)),
                dma((CHUNKS,)), dma((CHUNKS,)),
            ],
            compiler_params=pltpu.CompilerParams(
                collective_id=0, has_side_effects=True, vmem_limit_bytes=56 * 1024 * 1024),
            cost_estimate=pl.CostEstimate(
                flops=8 * R * T * C, bytes_accessed=8 * T * C, transcendentals=0),
        )(stream, short_taps, decay_rate, residue)

    in_specs = (P(None, "ctx", "dp"), P(), P("dp", None), P("dp", None))
    return jax.shard_map(shards, mesh=mesh, in_specs=in_specs, out_specs=P("ctx", "dp"), check_vma=False)
```

```python
import functools

import jax
import jax.numpy as jnp
from jax import lax
from jax.experimental import pallas as pl
from jax.experimental.pallas import tpu as pltpu
from jax.sharding import PartitionSpec as P

GROUP = 16
LANES = 128
CHUNKS = 4
PARTS = 2
DICT = pl.DeviceIdType.MESH


def kernel(
    n_ctx, n_dp,
    stream, taps, rate, resid, out,
    xv, tp, rates, resids, hs, hr, x0, prod, query, conv, sel, dec, amp, span, end, end_in,
    chain_in, other_in, chain_out, zs,
    local_sem, dp_send, dp_recv, halo_sem, end_send, end_recv, chain_send, chain_recv, fwd_send, fwd_recv,
):
    k = lax.axis_index("ctx")
    dp = lax.axis_index("dp")
    core = lax.rem(k, 2)
    z = k // 2
    last_z = n_ctx // 2 - 1
    partner = k + 1 - 2 * core
    T, C = stream.shape[1], stream.shape[2]
    J = C // LANES
    HJ = J // 2
    reach = taps.shape[1] - 1
    own_poles, G = rate.shape
    R = own_poles * n_dp
    RC = R // CHUNKS
    blocks = T // 16
    f32 = jnp.float32

    loads = []
    for n, i in enumerate((1, 2, 0)):
        loads.append(pltpu.make_async_copy(stream.at[i], xv.at[i], local_sem.at[n]))
    loads.append(pltpu.make_async_copy(taps.at[:, :, pl.ds(pl.multiple_of(dp * C, LANES), C)], tp, local_sem.at[3]))
    own_rate = pltpu.make_async_copy(rate, rates.at[dp], local_sem.at[4])
    own_resid = pltpu.make_async_copy(resid, resids.at[dp], local_sem.at[5])
    for c in loads:
        c.start()
    own_rate.start()
    own_resid.start()

    barrier = pltpu.get_barrier_semaphore()

    def greet(**where):
        pl.semaphore_signal(barrier, inc=1, device_id=where, device_id_type=DICT)

    for d in range(1, n_dp):
        greet(dp=lax.rem(dp + d, n_dp))
    greet(ctx=partner)
    beside = k - 1 + 2 * core
    has_beside = jnp.logical_and(beside >= 0, beside < n_ctx)
    has_prev, has_next = z > 0, z < last_z

    @pl.when(has_beside)
    def _():
        greet(ctx=beside)

    @pl.when(has_prev)
    def _():
        greet(ctx=k - 2)

    @pl.when(has_next)
    def _():
        greet(ctx=k + 2)

    pl.semaphore_wait(
        barrier,
        n_dp + has_beside.astype(jnp.int32) + has_prev.astype(jnp.int32) + has_next.astype(jnp.int32),
    )

    def dp_copy(which, d, owner, peer):
        dst = (rates, resids)[which]
        return pltpu.make_async_remote_copy(
            src_ref=dst.at[dp], dst_ref=dst.at[owner], send_sem=dp_send.at[which, d - 1],
            recv_sem=dp_recv.at[which, d - 1], device_id={"dp": peer}, device_id_type=DICT)

    own_rate.wait()
    own_resid.wait()
    for which in range(2):
        for d in range(1, n_dp):
            dp_copy(which, d, dp, lax.rem(dp + d, n_dp)).start()

    for c in loads:
        c.wait()
    for i in range(3):
        hs[i] = xv[i, T - 16:T, :].astype(f32)[16 - reach:16]

    def halo():
        return pltpu.make_async_remote_copy(
            src_ref=hs, dst_ref=hr, send_sem=halo_sem.at[0], recv_sem=halo_sem.at[1],
            device_id={"ctx": k + 1}, device_id_type=DICT)

    @pl.when(k < n_ctx - 1)
    def _():
        halo().start()

    def feature(i, j, window):
        cols = pl.ds(j * LANES, LANES)
        total = tp[i, 0:1, cols] * window[8:24]
        for lag in range(1, reach + 1):
            total = total + tp[i, lag:lag + 1, cols] * window[8 - lag:24 - lag]
        return total

    def window_at(i, j, b):
        cols = pl.ds(j * LANES, LANES)
        before = xv[i, pl.ds(pl.multiple_of(b * 16 - 16, 16), 16), cols].astype(f32)
        here = xv[i, pl.ds(pl.multiple_of(b * 16, 16), 16), cols].astype(f32)
        return jnp.concatenate([before[8:16], here], 0)

    def window_first(i, j):
        return x0[i, :, pl.ds(j * LANES, LANES)]

    def put(ref, b, j, tile):
        for u in range(2):
            ref[pl.ds(pl.multiple_of(((2 * b + u) * J + j) * 8, 8), 8), :] = tile[8 * u:8 * u + 8]

    @pl.loop(1, blocks)
    def _(b):
        for j in range(J):
            put(prod, b, j, feature(1, j, window_at(1, j, b)) * feature(2, j, window_at(2, j, b)))

    for d in range(1, n_dp):
        dp_copy(0, d, lax.rem(dp + n_dp - d, n_dp), dp).wait_recv()

    per_tile = LANES // GROUP
    groups = C // GROUP
    width = sel.shape[1]
    base = dp * groups
    window_start = base // width * width
    tile_of = (lax.broadcasted_iota(jnp.int32, (HJ, width), 1) - (base - window_start)) // per_tile
    row = lax.broadcasted_iota(jnp.int32, (HJ, width), 0)
    spread = (
        lax.rem(lax.broadcasted_iota(jnp.int32, (width, LANES), 0), per_tile)
        == lax.broadcasted_iota(jnp.int32, (width, LANES), 1) // GROUP
    ).astype(f32)
    shown = pl.ds(pl.multiple_of(window_start, LANES), width)

    def widen(source, use):
        for h in range(2):
            mask = tile_of == h * HJ + row
            for r in range(R):
                line = source[r // own_poles, r % own_poles:r % own_poles + 1, shown]
                sel[(h * R + r) * HJ:(h * R + r + 1) * HJ, :] = jnp.where(mask, line, 0.0)
        wide = jnp.dot(sel[...], spread, precision=lax.Precision.HIGHEST, preferred_element_type=f32)
        for h in range(2):
            for r in range(R):
                use(h, r, wide[(h * R + r) * HJ:(h * R + r + 1) * HJ])

    def use_rate(h, r, part):
        dec[h, r] = jnp.exp(-part)
        span[h, r] = jnp.exp(-part * T)

    def use_resid(h, r, part):
        amp[h, r] = part

    widen(rates, use_rate)

    @pl.when(k == 0)
    def _():
        hr[...] = jnp.zeros_like(hr)

    @pl.when(k > 0)
    def _():
        halo().wait_recv()

    for i in range(3):
        x0[i, 8 - reach:8, :] = hr[i]
        x0[i, 8:24, :] = xv[i, 0:16, :].astype(f32)
    for j in range(J):
        put(prod, 0, j, feature(1, j, window_first(1, j)) * feature(2, j, window_first(2, j)))

    def rows(tb, h, u):
        return pl.ds(tb * (J * 8) + h * (HJ * 8) + u, HJ, stride=8)

    RP = R // PARTS

    def close(part):
        slots = [(h, r) for h in range(2) for r in range(part * RP, (part + 1) * RP)]
        decay = [dec[h, r] for h, r in slots]

        def body(tb, state):
            for u in range(8):
                x = [prod[rows(tb, h, u), :] for h in range(2)]
                state = tuple(a * s + x[slot[0]] for slot, a, s in zip(slots, decay, state))
            return state

        state = lax.fori_loop(0, T // 8, body, tuple(jnp.zeros((HJ, LANES), f32) for _ in slots))
        for (h, r), value in zip(slots, state):
            end[h, r] = value

    def end_copy(h, part):
        piece = pl.ds(part * RP, RP)
        return pltpu.make_async_remote_copy(
            src_ref=end.at[h, piece], dst_ref=end_in.at[h, piece], send_sem=end_send.at[h, part],
            recv_sem=end_recv.at[h, part], device_id={"ctx": partner}, device_id_type=DICT)

    for part in range(PARTS):
        close(part)
        end_copy(1 - core, part).start()

    @pl.when(core == 0)
    def _():
        for part in range(PARTS):
            end_copy(0, part).start()

    def total_of_chip(part):
        end_copy(core, part).wait_recv()
        for r in range(part * RP, (part + 1) * RP):
            own, other = end[core, r], end_in[core, r]
            first = jnp.where(core == 0, own, other)
            second = jnp.where(core == 0, other, own)
            chain_out[r // RC, r % RC] = span[core, r] * first + second

    def chain_copy(c):
        return pltpu.make_async_remote_copy(
            src_ref=chain_out.at[c], dst_ref=chain_in.at[c], send_sem=chain_send.at[c],
            recv_sem=chain_recv.at[c], device_id={"ctx": k + 2}, device_id_type=DICT)

    def forward(c):
        return pltpu.make_async_remote_copy(
            src_ref=chain_in.at[c], dst_ref=other_in.at[c], send_sem=fwd_send.at[c],
            recv_sem=fwd_recv.at[c], device_id={"ctx": partner}, device_id_type=DICT)

    def relay():
        for c in range(CHUNKS):
            chain_copy(c).wait_recv()

            @pl.when(has_next)
            def _():
                for q in range(RC):
                    leap = span[core, c * RC + q]
                    chain_out[c, q] = chain_out[c, q] + leap * leap * chain_in[c, q]
                chain_copy(c).start()

            forward(c).start()

    for part in range(PARTS):
        total_of_chip(part)

        @pl.when(jnp.logical_and(z == 0, has_next))
        def _():
            for c in range(part * RP // RC, (part + 1) * RP // RC):
                chain_copy(c).start()

    @pl.when(z == 0)
    def _():
        chain_in[...] = jnp.zeros_like(chain_in)
        other_in[...] = jnp.zeros_like(other_in)

    for d in range(1, n_dp):
        dp_copy(1, d, lax.rem(dp + n_dp - d, n_dp), dp).wait_recv()
    widen(resids, use_resid)

    for j in range(J):
        put(query, 0, j, feature(0, j, window_first(0, j)))

    @pl.loop(1, blocks)
    def _(b):
        for j in range(J):
            put(query, b, j, feature(0, j, window_at(0, j, b)))

    def inside(h):
        decay = [dec[h, r] for r in range(R)]
        gain = [amp[h, r] for r in range(R)]

        def body(tb, state):
            for u in range(8):
                x = prod[rows(tb, h, u), :]
                state = tuple(a * s + x for a, s in zip(decay, state))
                terms = [g * s for g, s in zip(gain, state)]
                while len(terms) > 1:
                    terms = [sum(terms[n:n + 2][1:], terms[n]) for n in range(0, len(terms), 2)]
                conv[rows(tb, h, u), :] = terms[0]
            return state

        lax.fori_loop(0, T // 8, body, tuple(jnp.zeros((HJ, LANES), f32) for _ in range(R)))

    @pl.when(z == 1)
    def _():
        relay()

    inside(0)

    @pl.when(z == 2)
    def _():
        relay()

    inside(1)

    @pl.when(z > 2)
    def _():
        relay()

    @pl.when(core == 1)
    def _():
        for part in range(PARTS):
            end_copy(0, part).wait_recv()

    def tail(h, source):
        for r in range(R):
            zs[r] = source[r // RC, r % RC]

        @pl.when(core == 1)
        def _():
            for r in range(R):
                zs[r] = span[h, r] * zs[r] + end_in[h, r]

        decay = [dec[h, r] for r in range(R)]

        def body(tb, state):
            for u in range(8):
                state = tuple(a * s for a, s in zip(decay, state))
                terms = list(state)
                while len(terms) > 1:
                    terms = [sum(terms[n:n + 2][1:], terms[n]) for n in range(0, len(terms), 2)]
                conv[rows(tb, h, u), :] = conv[rows(tb, h, u), :] + terms[0]
            return state

        lax.fori_loop(0, T // 8, body, tuple(amp[h, r] * zs[r] for r in range(R)))

    def gate(h):
        @pl.loop(0, blocks)
        def _(b):
            for j in range(HJ):
                tiles = []
                for u in range(2):
                    at = pl.ds(pl.multiple_of(((2 * b + u) * J + h * HJ + j) * 8, 8), 8)
                    tiles.append(query[at, :] * conv[at, :])
                cols = pl.ds(pl.multiple_of((h * HJ + j) * LANES, LANES), LANES)
                out[pl.ds(pl.multiple_of(b * 16, 16), 16), cols] = jnp.concatenate(tiles, 0).astype(out.dtype)

    tail(core, chain_in)
    gate(core)

    @pl.when(has_prev)
    def _():
        for c in range(CHUNKS):
            forward(c).wait_recv()

    tail(1 - core, other_in)
    gate(1 - core)

    for d in range(1, n_dp):
        for which in range(2):
            dp_copy(which, d, dp, lax.rem(dp + d, n_dp)).wait_send()

    @pl.when(k < n_ctx - 1)
    def _():
        halo().wait_send()

    for part in range(PARTS):
        end_copy(1 - core, part).wait_send()

    @pl.when(core == 0)
    def _():
        for part in range(PARTS):
            end_copy(0, part).wait_send()

    for c in range(CHUNKS):
        @pl.when(has_next)
        def _():
            chain_copy(c).wait_send()

        @pl.when(has_prev)
        def _():
            forward(c).wait_send()


def solution(mesh):
    n_ctx, n_dp = mesh.shape["ctx"], mesh.shape["dp"]

    def shards(stream, short_taps, decay_rate, residue):
        T, C = stream.shape[1], stream.shape[2]
        n_taps = short_taps.shape[1]
        own_poles, G = decay_rate.shape
        R = own_poles * n_dp
        HJ = C // LANES // 2
        RC = R // CHUNKS
        f32 = jnp.float32
        dma = pltpu.SemaphoreType.DMA
        flat = pltpu.VMEM((T * C // LANES, LANES), f32)
        halves = pltpu.VMEM((2, R, HJ, LANES), f32)
        piece = pltpu.VMEM((CHUNKS, RC, HJ, LANES), f32)
        edge = pltpu.VMEM((3, n_taps - 1, C), f32)
        return pl.pallas_call(
            functools.partial(kernel, n_ctx, n_dp),
            out_shape=pltpu.VMEM((T, C), jnp.bfloat16),
            in_specs=[pl.BlockSpec(memory_space=pl.ANY)] * 4,
            out_specs=pl.BlockSpec(memory_space=pltpu.VMEM),
            scratch_shapes=[
                pltpu.VMEM((3, T, C), jnp.bfloat16),
                pltpu.VMEM((3, n_taps, C), f32),
                pltpu.VMEM((n_dp, own_poles, G), f32),
                pltpu.VMEM((n_dp, own_poles, G), f32),
                edge, edge,
                pltpu.VMEM((3, 24, C), f32),
                flat, flat, flat,
                pltpu.VMEM((2 * R * HJ, max(C // GROUP, LANES)), f32),
                halves, halves, halves, halves, halves,
                piece, piece, piece,
                pltpu.VMEM((R, HJ, LANES), f32),
                dma((6,)),
                dma((2, n_dp - 1)), dma((2, n_dp - 1)),
                dma((2,)),
                dma((2, PARTS)), dma((2, PARTS)),
                dma((CHUNKS,)), dma((CHUNKS,)),
                dma((CHUNKS,)), dma((CHUNKS,)),
            ],
            compiler_params=pltpu.CompilerParams(
                collective_id=0, has_side_effects=True, vmem_limit_bytes=56 * 1024 * 1024),
            cost_estimate=pl.CostEstimate(
                flops=8 * R * T * C, bytes_accessed=8 * T * C, transcendentals=0),
        )(stream, short_taps, decay_rate, residue)

    in_specs = (P(None, "ctx", "dp"), P(), P("dp", None), P("dp", None))
    return jax.shard_map(shards, mesh=mesh, in_specs=in_specs, out_specs=P("ctx", "dp"), check_vma=False)
```
